32 devices in a mesh: groups: 2 (over x), point: 8 (over z, y), dp: 2 (over core).
Axes of the slice: x: 2, y: 2, z: 4, core: 2. Of those that a mesh axis runs over, the one named last changes fastest.
Arguments:
- mesh_signals: bfloat16 [4, 32768, 256], P(('groups', 'dp'), 'point'), parts along dimension 0, may hold values from -40 to 40
- payload_linear_map: bfloat16 [256, 256], replicated, may hold values from -0.375 to 0.375
- partition_chooser_map: bfloat16 [256, 256], replicated, may hold values from -0.375 to 0.375
- partition_group_map: bfloat16 [32, 32], replicated, may hold values from -1 to 1
- softness_scale: float32 [8], replicated, may hold values from 0.25 to 1
- centroid_qkv_maps: bfloat16 [3, 32, 32], replicated, may hold values from -1 to 1
- final_linear_map: bfloat16 [256, 256], replicated, may hold values from -0.375 to 0.375
- final_shift_vector: float32 [256], replicated, may hold values from -3 to 3
- upstream_adjoint: bfloat16 [4, 32768, 256], P(('groups', 'dp'), 'point'), parts along dimension 0, may hold values from -6 to 6
Outputs:
- block_response: bfloat16 [4, 32768, 256], P(('groups', 'dp'), 'point'), parts along dimension 0
- input_signal_deriv: bfloat16 [4, 32768, 256], P(('groups', 'dp'), 'point'), parts along dimension 0
- payload_linear_deriv: float32 [512, 256], P('groups'), parts along dimension 0
- partition_chooser_deriv: float32 [512, 256], P('groups'), parts along dimension 0
- partition_group_deriv: float32 [64, 32], P('groups'), parts along dimension 0
- grad_token: float32 [6, 32, 32], P('groups'), parts along dimension 0
- softness_scale_deriv: float32 [16], P('groups'), parts along dimension 0
- final_linear_map_deriv: float32 [512, 256], P('groups'), parts along dimension 0
- shift_vector_deriv: float32 [512], P('groups'), parts along dimension 0
The draws below stay inside these ranges and needn't reach their ends.
There are 2 independent parts, one for each index of `groups`. The reference program is written for one: setup_inputs(seed, part) draws one part's arguments, and reference() takes and returns one part's arrays. A program takes and returns all parts, laid end to end along the dimension named above; an argument that names none is the same for every part. Nothing has to cross between parts.
All inputs are finite; a program needn't handle non-finite values.
Results may differ from the reference program's by a relative error of at most 0.012.
The reference program's roundings to bfloat16 on the way (of `values`, `weights_bf`, `attended_bf`, `mixed`, `d_mixed`, `d_numerator` and `d_values`) count: a program that leaves them out, or rounds other values in their place, can miss the bound.
Values sent between devices are 32-bit elements; how exact they have to be, the bound alone decides.
A program may use at most 128 MiB of HBM per device.

```python
import math
import jax
import jax.numpy as jnp
from jax import lax

C = 256
ATTN_GROUPS = 8
DH = 32
M = 32
POINTS = 32768
SAMPLES = 2


def draw_mesh_signals(key, part):
    key = jax.random.fold_in(key, 7)
    key_center, key_noise = jax.random.split(key, 2)
    places = jnp.arange(POINTS)
    region = places * 64 // POINTS
    centers = 1.5 * jax.random.normal(key_center, (SAMPLES, 64, C), jnp.float32)
    rising = 0.5 + places.astype(jnp.float32) / POINTS
    noise = jax.random.normal(key_noise, (SAMPLES, POINTS, C), jnp.float32)
    mixed = centers[:, region, :] + noise * rising[None, :, None]
    return jnp.clip(mixed, -40.0, 40.0).astype(jnp.bfloat16)


def level_of(own_key, dims, cuts, smallest, largest):
    level, own = 1.0, jax.random.fold_in(own_key, 6)
    for dim, blocks in cuts:
        draws = jnp.exp(jax.random.uniform(jax.random.fold_in(own, dim), (blocks,), jnp.float32, smallest / len(cuts), largest / len(cuts)))
        level = level * jnp.repeat(draws, dims[dim] // blocks).reshape([-1 if axis == dim else 1 for axis in range(len(dims))])
    return level


def bell_draw(key, extent, width, limit, cuts=(), dtype=jnp.bfloat16):
    values = jax.random.normal(key, extent, jnp.float32) * width
    if len(cuts) > 0:
        values = level_of(key, extent, cuts, -0.22, 0.18) * values
    return jnp.clip(values, min=-limit, max=limit).astype(dtype)


def setup_inputs(seed: int = 0, part: int = 0) -> dict:
    key_list = jax.random.split(jax.random.key(seed), 10)
    part_splits = jax.random.split(jax.random.fold_in(key_list[9], part), 10)
    mesh_signals = draw_mesh_signals(jax.random.fold_in(jax.random.fold_in(key_list[9], part), 71), part)
    payload_linear_map = bell_draw(key_list[1], (C, C), C ** -0.5, 0.375)
    partition_chooser_map = bell_draw(key_list[2], (C, C), C ** -0.5, 0.375)
    partition_group_map = bell_draw(key_list[3], (DH, M), DH ** -0.5, 1.0)
    softness_scale = jnp.clip(jnp.exp(jax.random.uniform(key_list[4], (ATTN_GROUPS,), jnp.float32, math.log(0.25), math.log(1.0))), 0.25, 1.0)
    centroid_qkv_maps = bell_draw(key_list[5], (3, DH, DH), DH ** -0.5, 1.0)
    final_linear_map = bell_draw(key_list[6], (C, C), C ** -0.5, 0.375)
    final_shift_vector = bell_draw(key_list[7], (C,), 0.5, 3.0, (), jnp.float32)
    upstream_adjoint = bell_draw(part_splits[8], (SAMPLES, POINTS, C), 1.0, 6.0, ((0, 2), (1, 8)))
    return {"mesh_signals": mesh_signals, "payload_linear_map": payload_linear_map, "partition_chooser_map": partition_chooser_map, "partition_group_map": partition_group_map, "softness_scale": softness_scale, "centroid_qkv_maps": centroid_qkv_maps, "final_linear_map": final_linear_map, "final_shift_vector": final_shift_vector, "upstream_adjoint": upstream_adjoint}


EPS = 1e-05
HIGH = lax.Precision.HIGHEST

def attend(tokens, matrices):
    query = jnp.einsum('shmd,de->shme', tokens, matrices[0], precision=HIGH)
    keys_all = jnp.einsum('shmd,de->shme', tokens, matrices[1], precision=HIGH)
    vals_all = jnp.einsum('shmd,de->shme', tokens, matrices[2], precision=HIGH)
    scores = jnp.einsum('shmd,shnd->shmn', query, keys_all, precision=HIGH) / math.sqrt(tokens.shape[-1])
    probs = jax.nn.softmax(scores, axis=-1)
    return jnp.einsum('shmn,shnd->shmd', probs, vals_all, precision=HIGH)

def reference(mesh_signals, payload_linear_map, partition_chooser_map, partition_group_map, softness_scale, centroid_qkv_maps, final_linear_map, final_shift_vector, upstream_adjoint):
    f32 = jnp.float32
    bf16 = jnp.bfloat16
    batch_extent, vertex_amount, channel_dimension = mesh_signals.shape
    group_index = softness_scale.shape[0]
    head_size = channel_dimension // group_index
    flat = mesh_signals.reshape(batch_extent * vertex_amount, channel_dimension)
    values = jnp.dot(flat, payload_linear_map, preferred_element_type=f32).astype(bf16).reshape(batch_extent, vertex_amount, group_index, head_size)
    chooser = jnp.dot(flat, partition_chooser_map, preferred_element_type=f32).reshape(batch_extent, vertex_amount, group_index, head_size)
    head_map = partition_group_map.astype(f32)
    plain_scores = jnp.einsum('sphd,dm->sphm', chooser, head_map, precision=HIGH)
    score_entry = plain_scores / softness_scale[:, None]
    weights = jax.nn.softmax(score_entry, axis=-1)
    weights_bf = weights.astype(bf16)
    numerator = jnp.einsum('sphm,sphd->shmd', weights_bf.astype(f32), values.astype(f32), precision=HIGH)
    weight_sum = lax.optimization_barrier(jnp.sum(weights, axis=1))
    reciprocal = 1.0 / (weight_sum + EPS)
    tokens = numerator * reciprocal[..., None]
    attended, attend_back = jax.vjp(attend, tokens, centroid_qkv_maps.astype(f32))
    attended_bf = attended.astype(bf16)
    mixed = jnp.einsum('sphm,shmd->sphd', weights_bf.astype(f32), attended_bf.astype(f32), precision=HIGH).astype(bf16)
    mixed_flat = mixed.reshape(batch_extent * vertex_amount, channel_dimension)
    block_response = (jnp.dot(mixed_flat, final_linear_map, preferred_element_type=f32) + final_shift_vector).astype(bf16)
    grad_flat = upstream_adjoint.reshape(batch_extent * vertex_amount, channel_dimension)
    shift_vector_deriv = lax.optimization_barrier(jnp.sum(grad_flat.astype(f32), axis=0))
    final_linear_map_deriv = jnp.dot(mixed_flat.T, grad_flat, preferred_element_type=f32)
    d_mixed = jnp.dot(grad_flat, final_linear_map.T, preferred_element_type=f32).astype(bf16).reshape(batch_extent, vertex_amount, group_index, head_size)
    d_attended = jnp.einsum('sphm,sphd->shmd', weights_bf.astype(f32), d_mixed.astype(f32), precision=HIGH)
    d_tokens, centroid_qkv_deriv = attend_back(d_attended)
    d_numerator = (d_tokens * reciprocal[..., None]).astype(bf16)
    d_weight_sum = -lax.optimization_barrier(jnp.sum(d_tokens * tokens, axis=-1)) * reciprocal
    d_weights = jnp.einsum('sphd,shmd->sphm', d_mixed.astype(f32), attended_bf.astype(f32), precision=HIGH)
    d_weights = d_weights + jnp.einsum('sphd,shmd->sphm', values.astype(f32), d_numerator.astype(f32), precision=HIGH)
    d_weights = d_weights + d_weight_sum[:, None]
    score_deriv = weights * (d_weights - lax.optimization_barrier(jnp.sum(weights * d_weights, axis=-1, keepdims=True)))
    direct_adjoint = score_deriv / softness_scale[:, None]
    softness_scale_deriv = -lax.optimization_barrier(jnp.sum(score_deriv * score_entry, axis=(0, 1, 3))) / softness_scale
    partition_group_deriv = jnp.einsum('sphd,sphm->dm', chooser, direct_adjoint, precision=HIGH)
    d_chooser = jnp.einsum('sphm,dm->sphd', direct_adjoint, head_map, precision=HIGH).astype(bf16).reshape(batch_extent * vertex_amount, channel_dimension)
    d_values = jnp.einsum('sphm,shmd->sphd', weights_bf.astype(f32), d_numerator.astype(f32), precision=HIGH).astype(bf16).reshape(batch_extent * vertex_amount, channel_dimension)
    input_signal_deriv = (jnp.dot(d_values, payload_linear_map.T, preferred_element_type=f32) + jnp.dot(d_chooser, partition_chooser_map.T, preferred_element_type=f32)).astype(bf16)
    payload_linear_deriv = jnp.dot(flat.T, d_values, preferred_element_type=f32)
    partition_chooser_deriv = jnp.dot(flat.T, d_chooser, preferred_element_type=f32)
    scaling_factor = 1.0 / math.sqrt(batch_extent * vertex_amount)
    return (block_response.reshape(batch_extent, vertex_amount, channel_dimension), input_signal_deriv.reshape(batch_extent, vertex_amount, channel_dimension), payload_linear_deriv * scaling_factor, partition_chooser_deriv * scaling_factor, partition_group_deriv * scaling_factor, centroid_qkv_deriv * scaling_factor, softness_scale_deriv * scaling_factor, final_linear_map_deriv * scaling_factor, shift_vector_deriv * scaling_factor)
```

```python
import functools
import math

import jax
import jax.numpy as jnp
from jax import lax
from jax.experimental import pallas as pl
from jax.experimental.pallas import tpu as pltpu
from jax.sharding import PartitionSpec as P

EPS = 1e-05
HIGH = lax.Precision.HIGHEST
F32 = jnp.float32
BF16 = jnp.bfloat16
VMEM_LIMIT = 56 * 1024 * 1024


def nt(a, b, precision=None):
    return lax.dot_general(
        a, b, (((1,), (1,)), ((), ())), precision=precision, preferred_element_type=F32
    )


def nn(a, b, precision=None):
    return lax.dot_general(
        a, b, (((1,), (0,)), ((), ())), precision=precision, preferred_element_type=F32
    )


def tn(a, b, precision=None):
    return lax.dot_general(
        a, b, (((0,), (0,)), ((), ())), precision=precision, preferred_element_type=F32
    )


def block_mask(size, head):
    row = lax.broadcasted_iota(jnp.int32, (size, size), 0) // head
    col = lax.broadcasted_iota(jnp.int32, (size, size), 1) // head
    return row == col


def fold(square, mask, heads, head):
    kept = jnp.where(mask, square, 0.0)
    return jnp.sum(kept.reshape(heads, head, heads * head), axis=0)


def unfold(flat, mask, heads):
    return jnp.where(mask, jnp.concatenate([flat] * heads, axis=0), 0.0)


def forward_kernel(
    heads, x_ref, u_ref, wp_ref, hi_ref, lo_ref, wf_ref, vt_ref, wt_ref, dmt_ref, sums_ref, acc, wacc
):
    step = pl.program_id(0)
    size, rows = wt_ref.shape
    head = size // heads
    x = x_ref[...]
    values = nt(wp_ref[...], x).astype(BF16)
    logit = nt(hi_ref[...], x) + nt(lo_ref[...], x)
    d_mixed = nt(wf_ref[...], u_ref[...]).astype(BF16)
    logit = logit.reshape(heads, head, rows)
    top = jnp.max(logit, axis=1, keepdims=True)
    grown = jnp.exp(logit - top)
    share = 1.0 / jnp.sum(grown, axis=1, keepdims=True)
    weights = (grown * share).reshape(size, rows)
    weights_bf = weights.astype(BF16)
    vt_ref[...] = values
    dmt_ref[...] = d_mixed
    wt_ref[...] = weights
    both = nt(weights_bf, jnp.concatenate([values, d_mixed], axis=0))
    lanes = wacc.shape[1]
    part = weights[:, :lanes]
    for i in range(1, rows // lanes):
        part = part + weights[:, i * lanes : (i + 1) * lanes]

    @pl.when(step == 0)
    def _():
        acc[...] = both
        wacc[...] = part

    @pl.when(step > 0)
    def _():
        acc[...] += both
        wacc[...] += part

    @pl.when(step == pl.num_programs(0) - 1)
    def _():
        mask = block_mask(size, head)
        total = jnp.sum(wacc[...], axis=1, keepdims=True)
        sums_ref[0:head, :] = fold(acc[:, :size], mask, heads, head)
        sums_ref[head : 2 * head, :] = fold(acc[:, size:], mask, heads, head)
        sums_ref[2 * head : 3 * head, :] = fold(
            jnp.broadcast_to(total, (size, size)), mask, heads, head
        )
        spare = sums_ref.shape[0] - 3 * head
        if spare:
            sums_ref[3 * head :, :] = jnp.zeros((spare, size), F32)


def token_kernel(heads, sums_ref, maps_ref, att_ref, dnum_ref, dws_ref, dmap_ref):
    size = maps_ref.shape[1]
    head = size // heads
    mask = block_mask(size, head)
    numerator = unfold(sums_ref[0:head, :], mask, heads)
    d_att = unfold(sums_ref[head : 2 * head, :], mask, heads)
    spread = unfold(sums_ref[2 * head : 3 * head, :], mask, heads)
    weight_sum = jnp.sum(spread, axis=1, keepdims=True) * (1.0 / head)
    reciprocal = 1.0 / (weight_sum + EPS)
    tokens = numerator * reciprocal
    maps = [maps_ref[i] for i in range(3)]
    q, k, v = (nn(tokens, w, HIGH) for w in maps)
    root = 1.0 / math.sqrt(head)
    scores = jnp.where(mask, nt(q, k, HIGH) * root, -jnp.inf)
    grown = jnp.exp(scores - jnp.max(scores, axis=1, keepdims=True))
    probs = grown / jnp.sum(grown, axis=1, keepdims=True)
    attended = nn(probs, v, HIGH)
    d_v = tn(probs, d_att, HIGH)
    d_probs = nt(d_att, v, HIGH)
    d_scores = probs * (d_probs - jnp.sum(probs * d_probs, axis=1, keepdims=True)) * root
    d_q = nn(d_scores, k, HIGH)
    d_k = tn(d_scores, q, HIGH)
    d_tokens = nt(d_q, maps[0], HIGH) + nt(d_k, maps[1], HIGH) + nt(d_v, maps[2], HIGH)
    att_ref[...] = attended.astype(BF16)
    dnum_ref[...] = (d_tokens * reciprocal).astype(BF16)
    dws = -jnp.sum(d_tokens * tokens, axis=1, keepdims=True) * reciprocal
    dws_ref[...] = jnp.broadcast_to(dws, dws_ref.shape)
    for i, d in enumerate((d_q, d_k, d_v)):
        dmap_ref[i] = fold(tn(tokens, d, HIGH), mask, heads, head)


def backward_kernel(
    heads, points,
    x_ref, u_ref, vt_ref, wt_ref, dmt_ref, att_ref, dnum_ref, dws_ref,
    wp_ref, hi_ref, lo_ref, wf_ref, shift_ref, dmap_ref,
    resp_ref, din_ref, grads_ref,
):
    step = pl.program_id(0)
    size, rows = wt_ref.shape
    head = size // heads
    u = u_ref[...]
    x = x_ref[...]
    weights = wt_ref[...]
    weights_bf = weights.astype(BF16)
    mixed = tn(att_ref[...], weights_bf).astype(BF16)
    d_values = tn(dnum_ref[...], weights_bf).astype(BF16)
    resp_ref[...] = (tn(mixed, wf_ref[...]) + shift_ref[...]).astype(BF16)
    d_weights = nn(att_ref[...], dmt_ref[...]) + nn(dnum_ref[...], vt_ref[...])
    d_weights = d_weights + dws_ref[:, 0:1]
    product = (weights * d_weights).reshape(heads, head, rows)
    mean = jnp.sum(product, axis=1, keepdims=True)
    d_logit = (product - weights.reshape(heads, head, rows) * mean).reshape(size, rows)
    d_high = d_logit.astype(BF16)
    d_low = (d_logit - d_high.astype(F32)).astype(BF16)
    din_ref[...] = (
        tn(d_values, wp_ref[...])
        + tn(d_high, hi_ref[...])
        + tn(d_high, lo_ref[...])
        + tn(d_low, hi_ref[...])
    ).astype(BF16)
    ones = jnp.ones((8, rows), BF16)
    parts = (nn(d_values, x), nn(d_high, x) + nn(d_low, x), nn(mixed, u), nn(ones, u))
    spans = ((0, size), (size, 2 * size), (2 * size, 3 * size), (3 * size, 3 * size + 8))

    @pl.when(step == 0)
    def _():
        for (a, b), part in zip(spans, parts):
            grads_ref[a:b, :] = part
        tail = 3 * size + 8
        end = tail + 3 * head
        grads_ref[tail:end, :] = dmap_ref[...] * (1.0 / points)
        spare = grads_ref.shape[0] - end
        if spare:
            grads_ref[end:, :] = jnp.zeros((spare, size), F32)

    @pl.when(step > 0)
    def _():
        for (a, b), part in zip(spans, parts):
            grads_ref[a:b, :] += part


def reduce_kernel(n, paired, x_ref, out_ref, recv, full, rs_sem, ag_sem, *more):
    me = lax.axis_index("point")
    core = lax.axis_index("dp")
    peers = [lax.rem(me + o, n) for o in range(1, n)]
    mesh_id = pl.DeviceIdType.MESH
    barrier = pltpu.get_barrier_semaphore()
    for peer in peers:
        pl.semaphore_signal(barrier, inc=1, device_id={"point": peer}, device_id_type=mesh_id)
    if paired:
        pl.semaphore_signal(barrier, inc=1, device_id={"dp": 1 - core}, device_id_type=mesh_id)
    pl.semaphore_wait(barrier, n if paired else n - 1)

    def send(src, dst, sems, slot, target):
        copy = pltpu.make_async_remote_copy(
            src_ref=src, dst_ref=dst, send_sem=sems.at[0, slot], recv_sem=sems.at[1, slot],
            device_id=target, device_id_type=mesh_id,
        )
        copy.start()
        return copy

    if paired:
        swapped, half, swap_sem, pass_sem = more
        swaps = [
            send(x_ref.at[1 - core, k], swapped.at[k], swap_sem, k, {"dp": 1 - core})
            for k in range(n)
        ]
        for k in range(n):
            swaps[k].wait_recv()
            half[k] = x_ref[core, k] + swapped[k]
        source, target = half, full.at[core]
    else:
        source, target = x_ref, full
    scatter = [
        send(source.at[peer], recv.at[o], rs_sem, o, {"point": peer})
        for o, peer in enumerate(peers)
    ]
    total = source[me]
    for o, copy in enumerate(scatter):
        copy.wait_recv()
        total = total + recv[o]
    target[me] = total
    gather = [
        send(target.at[me], target.at[me], ag_sem, o, {"point": peer})
        for o, peer in enumerate(peers)
    ]
    passed = []
    if paired:
        passed.append(send(target.at[me], target.at[me], pass_sem, 0, {"dp": 1 - core}))
    for o, copy in enumerate(gather):
        copy.wait_recv()
        if paired:
            owner = lax.rem(me + n - (o + 1), n)
            passed.append(
                send(target.at[owner], target.at[owner], pass_sem, o + 1, {"dp": 1 - core})
            )
    if paired:
        for copy in passed:
            copy.wait_recv()
        for copy in swaps + passed:
            copy.wait_send()
    for copy in scatter + gather:
        copy.wait_send()
    out_ref[...] = full[...]


def reduce_over(x, n, paired):
    rows, size = x.shape
    r = rows // (2 * n if paired else n)
    shape = (2, n, r, size) if paired else (n, r, size)
    dma = pltpu.SemaphoreType.DMA
    scratch = [
        pltpu.VMEM((n - 1, r, size), F32), pltpu.VMEM(shape, F32), dma((2, n - 1)), dma((2, n - 1)),
    ]
    if paired:
        scratch += [
            pltpu.VMEM((n, r, size), F32), pltpu.VMEM((n, r, size), F32), dma((2, n)), dma((2, n)),
        ]
    out = pl.pallas_call(
        functools.partial(reduce_kernel, n, paired),
        out_shape=jax.ShapeDtypeStruct(shape, F32),
        in_specs=[pl.BlockSpec(memory_space=pltpu.VMEM)],
        out_specs=pl.BlockSpec(memory_space=pltpu.VMEM),
        scratch_shapes=scratch,
        compiler_params=pltpu.CompilerParams(
            collective_id=1 if paired else 0, has_side_effects=True, vmem_limit_bytes=VMEM_LIMIT
        ),
    )(x.reshape(shape))
    return out.reshape(rows, size)


def padded(rows, pieces):
    return pieces * 8 * -(-rows // (pieces * 8))


def spread_heads(small, heads):
    return jnp.kron(jnp.eye(heads, dtype=small.dtype), small)


def shards(
    mesh_signals,
    payload_linear_map,
    partition_chooser_map,
    partition_group_map,
    softness_scale,
    centroid_qkv_maps,
    final_linear_map,
    final_shift_vector,
    upstream_adjoint,
):
    batch, points, size = mesh_signals.shape
    heads = softness_scale.shape[0]
    head = size // heads
    x = mesh_signals.reshape(points, size)
    u = upstream_adjoint.reshape(points, size)
    rows = 512
    steps = points // rows
    n_point = lax.axis_size("point")
    sum_rows = padded(3 * head, n_point)
    grad_rows = padded(3 * size + 8 + 3 * head, 2 * n_point)
    inverse = jnp.repeat(1.0 / softness_scale, head)
    group_square = spread_heads(partition_group_map.astype(F32), heads)
    joined = jnp.dot(partition_chooser_map.astype(F32), group_square, precision=HIGH) * inverse
    joined_t = joined.T
    rounded = lax.reduce_precision(joined_t, 8, 7)
    hi = rounded.astype(BF16)
    lo = (joined_t - rounded).astype(BF16)
    params = pltpu.CompilerParams(
        dimension_semantics=("arbitrary",), vmem_limit_bytes=VMEM_LIMIT
    )
    tall = pl.BlockSpec((rows, size), lambda i: (i, 0))
    wide = pl.BlockSpec((size, rows), lambda i: (0, i))

    def whole(*shape):
        return pl.BlockSpec(shape, lambda i: (0,) * len(shape))

    square = whole(size, size)
    vt, wt, dmt, sums = pl.pallas_call(
        functools.partial(forward_kernel, heads),
        grid=(steps,),
        in_specs=[tall, tall, square, square, square, square],
        out_specs=[wide, wide, wide, whole(sum_rows, size)],
        out_shape=[
            jax.ShapeDtypeStruct((size, points), BF16),
            jax.ShapeDtypeStruct((size, points), F32),
            jax.ShapeDtypeStruct((size, points), BF16),
            jax.ShapeDtypeStruct((sum_rows, size), F32),
        ],
        scratch_shapes=[pltpu.VMEM((size, 2 * size), F32), pltpu.VMEM((size, 128), F32)],
        compiler_params=params,
    )(x, u, payload_linear_map.T, hi, lo, final_linear_map)
    sums = reduce_over(sums, n_point, False)
    maps = jnp.stack([spread_heads(centroid_qkv_maps[i].astype(F32), heads) for i in range(3)])
    att, dnum, dws, dmap = pl.pallas_call(
        functools.partial(token_kernel, heads),
        out_shape=[
            jax.ShapeDtypeStruct((size, size), BF16),
            jax.ShapeDtypeStruct((size, size), BF16),
            jax.ShapeDtypeStruct((size, 128), F32),
            jax.ShapeDtypeStruct((3, head, size), F32),
        ],
        compiler_params=pltpu.CompilerParams(vmem_limit_bytes=VMEM_LIMIT),
    )(sums, maps)
    resp, din, grads = pl.pallas_call(
        functools.partial(backward_kernel, heads, n_point),
        grid=(steps,),
        in_specs=[
            tall, tall, wide, wide, wide, square, square, whole(size, 128),
            square, square, square, square, whole(1, size), whole(3 * head, size),
        ],
        out_specs=[tall, tall, whole(grad_rows, size)],
        out_shape=[
            jax.ShapeDtypeStruct((points, size), BF16),
            jax.ShapeDtypeStruct((points, size), BF16),
            jax.ShapeDtypeStruct((grad_rows, size), F32),
        ],
        compiler_params=params,
    )(
        x, u, vt, wt, dmt, att, dnum, dws,
        payload_linear_map.T, hi, lo, final_linear_map, final_shift_vector[None, :],
        dmap.reshape(3 * head, size),
    )
    grads = reduce_over(grads, n_point, True)
    tail = 3 * size + 8
    d_maps = jnp.sum(grads[tail : tail + 3 * head].reshape(3, head, heads, head), axis=2)
    scaling = 1.0 / math.sqrt(
        batch * points * lax.axis_size("point") * lax.axis_size("dp")
    )
    payload_deriv = grads[:size].T * scaling
    logit_deriv = grads[size : 2 * size].T
    raw_deriv = logit_deriv * (inverse * scaling)
    chooser_deriv = jnp.dot(raw_deriv, group_square.T, precision=HIGH)
    crossed = jnp.dot(partition_chooser_map.astype(F32).T, raw_deriv, precision=HIGH)
    crossed = crossed.reshape(heads, head, heads, head)
    group_deriv = sum(crossed[h, :, h] for h in range(heads))
    softness_deriv = -scaling * jnp.sum((joined * logit_deriv).reshape(size, heads, head), axis=(0, 2))
    softness_deriv = softness_deriv / softness_scale
    return (
        resp.reshape(batch, points, size),
        din.reshape(batch, points, size),
        payload_deriv,
        chooser_deriv,
        group_deriv,
        d_maps * scaling,
        softness_deriv,
        grads[2 * size : 3 * size] * scaling,
        grads[3 * size] * scaling,
    )


def solution(mesh):
    placed = (
        P(("groups", "dp"), "point", None),
        P(),
        P(),
        P(),
        P(),
        P(),
        P(),
        P(),
        P(("groups", "dp"), "point", None),
    )
    return jax.shard_map(
        shards,
        mesh=mesh,
        in_specs=placed,
        out_specs=(
            P(("groups", "dp"), "point", None),
            P(("groups", "dp"), "point", None),
            P("groups", None),
            P("groups", None),
            P("groups", None),
            P("groups", None, None),
            P("groups"),
            P("groups", None),
            P("groups"),
        ),
        check_vma=False,
    )
```

```python
import functools
import math

import jax
import jax.numpy as jnp
from jax import lax
from jax.experimental import pallas as pl
from jax.experimental.pallas import tpu as pltpu
from jax.sharding import PartitionSpec as P

EPS = 1e-05
HIGH = lax.Precision.HIGHEST
F32 = jnp.float32
BF16 = jnp.bfloat16
VMEM_LIMIT = 56 * 1024 * 1024


def nt(a, b, precision=None):
    return lax.dot_general(
        a, b, (((1,), (1,)), ((), ())), precision=precision, preferred_element_type=F32
    )


def nn(a, b, precision=None):
    return lax.dot_general(
        a, b, (((1,), (0,)), ((), ())), precision=precision, preferred_element_type=F32
    )


def tn(a, b, precision=None):
    return lax.dot_general(
        a, b, (((0,), (0,)), ((), ())), precision=precision, preferred_element_type=F32
    )


def block_mask(size, head):
    row = lax.broadcasted_iota(jnp.int32, (size, size), 0) // head
    col = lax.broadcasted_iota(jnp.int32, (size, size), 1) // head
    return row == col


def fold(square, mask, heads, head):
    kept = jnp.where(mask, square, 0.0)
    return jnp.sum(kept.reshape(heads, head, heads * head), axis=0)


def unfold(flat, mask, heads):
    return jnp.where(mask, jnp.concatenate([flat] * heads, axis=0), 0.0)


def pick(size, head, dtype):
    row = lax.broadcasted_iota(jnp.int32, (size, head), 0)
    col = lax.broadcasted_iota(jnp.int32, (size, head), 1)
    return jnp.where(row % head == col, 1.0, 0.0).astype(dtype)


def head_column(scale_row, size, head):
    heads = size // head
    row = lax.broadcasted_iota(jnp.int32, (size, heads), 0) // head
    mine = row == lax.broadcasted_iota(jnp.int32, (size, heads), 1)
    return jnp.sum(jnp.where(mine, scale_row, 0.0), axis=1, keepdims=True), mine


def square_transposed(group, size, head):
    e = pick(size, head, BF16)
    return jnp.where(block_mask(size, head), nt(nt(e, group).astype(BF16), e), 0.0)


def forward_kernel(
    heads, x_ref, u_ref, payload_ref, chooser_ref, group_ref, scale_ref, wf_ref,
    vt_ref, wt_ref, dmt_ref, sums_ref, wp_ref, hi_ref, lo_ref, acc, wacc
):
    step = pl.program_id(0)
    size, rows = wt_ref.shape
    head = size // heads

    @pl.when(step == 0)
    def _():
        row = lax.broadcasted_iota(jnp.int32, (size, size), 0)
        col = lax.broadcasted_iota(jnp.int32, (size, size), 1)
        same = jnp.where(row == col, 1.0, 0.0).astype(BF16)
        wp_ref[...] = nt(same, payload_ref[...]).astype(BF16)
        group_t = square_transposed(group_ref[...], size, head).astype(BF16)
        column, _ = head_column(scale_ref[...], size, head)
        joined = nt(group_t, chooser_ref[...]) / column
        high = joined.astype(BF16)
        hi_ref[...] = high
        lo_ref[...] = (joined - high.astype(F32)).astype(BF16)

    x = x_ref[...]
    values = nt(wp_ref[...], x).astype(BF16)
    logit = nt(hi_ref[...], x) + nt(lo_ref[...], x)
    d_mixed = nt(wf_ref[...], u_ref[...]).astype(BF16)
    logit = logit.reshape(heads, head, rows)
    top = jnp.max(logit, axis=1, keepdims=True)
    grown = jnp.exp(logit - top)
    share = 1.0 / jnp.sum(grown, axis=1, keepdims=True)
    weights = (grown * share).reshape(size, rows)
    weights_bf = weights.astype(BF16)
    vt_ref[...] = values
    dmt_ref[...] = d_mixed
    wt_ref[...] = weights
    both = nt(weights_bf, jnp.concatenate([values, d_mixed], axis=0))
    lanes = wacc.shape[1]
    part = weights[:, :lanes]
    for i in range(1, rows // lanes):
        part = part + weights[:, i * lanes : (i + 1) * lanes]

    @pl.when(step == 0)
    def _():
        acc[...] = both
        wacc[...] = part

    @pl.when(step > 0)
    def _():
        acc[...] += both
        wacc[...] += part

    @pl.when(step == pl.num_programs(0) - 1)
    def _():
        mask = block_mask(size, head)
        total = jnp.sum(wacc[...], axis=1, keepdims=True)
        sums_ref[0:head, :] = fold(acc[:, :size], mask, heads, head)
        sums_ref[head : 2 * head, :] = fold(acc[:, size:], mask, heads, head)
        sums_ref[2 * head : 3 * head, :] = fold(
            jnp.broadcast_to(total, (size, size)), mask, heads, head
        )
        spare = sums_ref.shape[0] - 3 * head
        if spare:
            sums_ref[3 * head :, :] = jnp.zeros((spare, size), F32)


def token_kernel(heads, sums_ref, maps_ref, att_ref, dnum_ref, dws_ref, dmap_ref):
    size = sums_ref.shape[1]
    head = size // heads
    mask = block_mask(size, head)
    numerator = unfold(sums_ref[0:head, :], mask, heads)
    d_att = unfold(sums_ref[head : 2 * head, :], mask, heads)
    spread = unfold(sums_ref[2 * head : 3 * head, :], mask, heads)
    weight_sum = jnp.sum(spread, axis=1, keepdims=True) * (1.0 / head)
    reciprocal = 1.0 / (weight_sum + EPS)
    tokens = numerator * reciprocal
    e = pick(size, head, BF16)
    maps = [
        jnp.where(mask, nt(nn(e, maps_ref[i]).astype(BF16), e), 0.0) for i in range(3)
    ]
    q, k, v = (nn(tokens, w, HIGH) for w in maps)
    root = 1.0 / math.sqrt(head)
    scores = jnp.where(mask, nt(q, k, HIGH) * root, -jnp.inf)
    grown = jnp.exp(scores - jnp.max(scores, axis=1, keepdims=True))
    probs = grown / jnp.sum(grown, axis=1, keepdims=True)
    attended = nn(probs, v, HIGH)
    d_v = tn(probs, d_att, HIGH)
    d_probs = nt(d_att, v, HIGH)
    d_scores = probs * (d_probs - jnp.sum(probs * d_probs, axis=1, keepdims=True)) * root
    d_q = nn(d_scores, k, HIGH)
    d_k = tn(d_scores, q, HIGH)
    d_tokens = nt(d_q, maps[0], HIGH) + nt(d_k, maps[1], HIGH) + nt(d_v, maps[2], HIGH)
    att_ref[...] = attended.astype(BF16)
    dnum_ref[...] = (d_tokens * reciprocal).astype(BF16)
    dws = -jnp.sum(d_tokens * tokens, axis=1, keepdims=True) * reciprocal
    dws_ref[...] = jnp.broadcast_to(dws, dws_ref.shape)
    for i, d in enumerate((d_q, d_k, d_v)):
        dmap_ref[i] = fold(tn(tokens, d, HIGH), mask, heads, head)


def backward_kernel(
    heads, points,
    x_ref, u_ref, vt_ref, wt_ref, dmt_ref, att_ref, dnum_ref, dws_ref,
    wp_ref, hi_ref, lo_ref, wf_ref, shift_ref, dmap_ref,
    resp_ref, din_ref, grads_ref,
):
    step = pl.program_id(0)
    size, rows = wt_ref.shape
    head = size // heads
    u = u_ref[...]
    x = x_ref[...]
    weights = wt_ref[...]
    weights_bf = weights.astype(BF16)
    mixed = tn(att_ref[...], weights_bf).astype(BF16)
    d_values = tn(dnum_ref[...], weights_bf).astype(BF16)
    resp_ref[...] = (tn(mixed, wf_ref[...]) + shift_ref[...]).astype(BF16)
    d_weights = nn(att_ref[...], dmt_ref[...]) + nn(dnum_ref[...], vt_ref[...])
    d_weights = d_weights + dws_ref[:, 0:1]
    product = (weights * d_weights).reshape(heads, head, rows)
    mean = jnp.sum(product, axis=1, keepdims=True)
    d_logit = (product - weights.reshape(heads, head, rows) * mean).reshape(size, rows)
    d_high = d_logit.astype(BF16)
    d_low = (d_logit - d_high.astype(F32)).astype(BF16)
    din_ref[...] = (
        tn(d_values, wp_ref[...])
        + tn(d_high, hi_ref[...])
        + tn(d_high, lo_ref[...])
        + tn(d_low, hi_ref[...])
    ).astype(BF16)
    ones = jnp.ones((8, rows), BF16)
    parts = (nn(d_values, x), nn(d_high, x) + nn(d_low, x), nn(mixed, u), nn(ones, u))
    spans = ((0, size), (size, 2 * size), (2 * size, 3 * size), (3 * size, 3 * size + 8))

    @pl.when(step == 0)
    def _():
        for (a, b), part in zip(spans, parts):
            grads_ref[a:b, :] = part
        tail = 3 * size + 8
        end = tail + 3 * head
        grads_ref[tail:end, :] = dmap_ref[...] * (1.0 / points)
        spare = grads_ref.shape[0] - end
        if spare:
            grads_ref[end:, :] = jnp.zeros((spare, size), F32)

    @pl.when(step > 0)
    def _():
        for (a, b), part in zip(spans, parts):
            grads_ref[a:b, :] += part


def reduce_kernel(n, paired, x_ref, out_ref, recv, full, rs_sem, ag_sem, *more):
    me = lax.axis_index("point")
    core = lax.axis_index("dp")
    peers = [lax.rem(me + o, n) for o in range(1, n)]
    mesh_id = pl.DeviceIdType.MESH
    barrier = pltpu.get_barrier_semaphore()
    for peer in peers:
        pl.semaphore_signal(barrier, inc=1, device_id={"point": peer}, device_id_type=mesh_id)
    if paired:
        pl.semaphore_signal(barrier, inc=1, device_id={"dp": 1 - core}, device_id_type=mesh_id)
    pl.semaphore_wait(barrier, n if paired else n - 1)

    def send(src, dst, sems, slot, target):
        copy = pltpu.make_async_remote_copy(
            src_ref=src, dst_ref=dst, send_sem=sems.at[0, slot], recv_sem=sems.at[1, slot],
            device_id=target, device_id_type=mesh_id,
        )
        copy.start()
        return copy

    if paired:
        swapped, half, swap_sem, pass_sem = more
        swaps = [
            send(x_ref.at[1 - core, k], swapped.at[k], swap_sem, k, {"dp": 1 - core})
            for k in range(n)
        ]
        for k in range(n):
            swaps[k].wait_recv()
            half[k] = x_ref[core, k] + swapped[k]
        source, target = half, full.at[core]
    else:
        source, target = x_ref, full
    scatter = [
        send(source.at[peer], recv.at[o], rs_sem, o, {"point": peer})
        for o, peer in enumerate(peers)
    ]
    total = source[me]
    for o, copy in enumerate(scatter):
        copy.wait_recv()
        total = total + recv[o]
    target[me] = total
    gather = [
        send(target.at[me], target.at[me], ag_sem, o, {"point": peer})
        for o, peer in enumerate(peers)
    ]
    passed = []
    if paired:
        passed.append(send(target.at[me], target.at[me], pass_sem, 0, {"dp": 1 - core}))
    for o, copy in enumerate(gather):
        copy.wait_recv()
        if paired:
            owner = lax.rem(me + n - (o + 1), n)
            passed.append(
                send(target.at[owner], target.at[owner], pass_sem, o + 1, {"dp": 1 - core})
            )
    if paired:
        for copy in passed:
            copy.wait_recv()
        for copy in swaps + passed:
            copy.wait_send()
    for copy in scatter + gather:
        copy.wait_send()
    out_ref[...] = full[...]


def reduce_over(x, n, paired):
    rows, size = x.shape
    r = rows // (2 * n if paired else n)
    shape = (2, n, r, size) if paired else (n, r, size)
    dma = pltpu.SemaphoreType.DMA
    scratch = [
        pltpu.VMEM((n - 1, r, size), F32), pltpu.VMEM(shape, F32), dma((2, n - 1)), dma((2, n - 1)),
    ]
    if paired:
        scratch += [
            pltpu.VMEM((n, r, size), F32), pltpu.VMEM((n, r, size), F32), dma((2, n)), dma((2, n)),
        ]
    out = pl.pallas_call(
        functools.partial(reduce_kernel, n, paired),
        out_shape=jax.ShapeDtypeStruct(shape, F32),
        in_specs=[pl.BlockSpec(memory_space=pltpu.VMEM)],
        out_specs=pl.BlockSpec(memory_space=pltpu.VMEM),
        scratch_shapes=scratch,
        compiler_params=pltpu.CompilerParams(
            collective_id=1 if paired else 0, has_side_effects=True, vmem_limit_bytes=VMEM_LIMIT
        ),
    )(x.reshape(shape))
    return out.reshape(rows, size)


def padded(rows, pieces):
    return pieces * 8 * -(-rows // (pieces * 8))


def finish_kernel(
    heads, scaling, grads_ref, hi_ref, lo_ref, chooser_ref, group_ref, scale_ref,
    payload_out, chooser_out, group_out, maps_out, softness_out, final_out, shift_out,
):
    size = grads_ref.shape[1]
    head = size // heads
    mask = block_mask(size, head)
    e = pick(size, head, F32)
    payload_out[...] = grads_ref[0:size, :].T * scaling
    logit_deriv = grads_ref[size : 2 * size, :]
    column, mine = head_column(scale_ref[...], size, head)
    raw_deriv = logit_deriv * (scaling / column)
    group_t = square_transposed(group_ref[...], size, head)
    chooser_out[...] = tn(raw_deriv, group_t, HIGH)
    crossed = jnp.where(mask, nn(raw_deriv, chooser_ref[...].astype(F32), HIGH), 0.0)
    group_out[...] = tn(e, tn(crossed, e, HIGH), HIGH)
    joined = hi_ref[...].astype(F32) + lo_ref[...].astype(F32)
    per_row = jnp.sum(joined * logit_deriv, axis=1, keepdims=True)
    per_head = jnp.sum(jnp.where(mine, per_row, 0.0), axis=0, keepdims=True)
    softness_out[...] = -scaling * per_head / scale_ref[...]
    final_out[...] = grads_ref[2 * size : 3 * size, :] * scaling
    shift_out[...] = grads_ref[3 * size : 3 * size + 1, :] * scaling
    tail = 3 * size + 8
    maps_out[...] = nn(grads_ref[tail : tail + 3 * head, :], e, HIGH) * scaling


def shards(
    mesh_signals,
    payload_linear_map,
    partition_chooser_map,
    partition_group_map,
    softness_scale,
    centroid_qkv_maps,
    final_linear_map,
    final_shift_vector,
    upstream_adjoint,
):
    batch, points, size = mesh_signals.shape
    heads = softness_scale.shape[0]
    head = size // heads
    x = mesh_signals.reshape(points, size)
    u = upstream_adjoint.reshape(points, size)
    rows = 512
    steps = points // rows
    n_point = lax.axis_size("point")
    sum_rows = padded(3 * head, n_point)
    grad_rows = padded(3 * size + 8 + 3 * head, 2 * n_point)
    scale_row = softness_scale[None, :]
    params = pltpu.CompilerParams(
        dimension_semantics=("arbitrary",), vmem_limit_bytes=VMEM_LIMIT
    )
    tall = pl.BlockSpec((rows, size), lambda i: (i, 0))
    wide = pl.BlockSpec((size, rows), lambda i: (0, i))

    def whole(*shape):
        return pl.BlockSpec(shape, lambda i: (0,) * len(shape))

    square = whole(size, size)
    vt, wt, dmt, sums, wp, hi, lo = pl.pallas_call(
        functools.partial(forward_kernel, heads),
        grid=(steps,),
        in_specs=[
            tall, tall, square, square, whole(head, head), whole(1, heads), square,
        ],
        out_specs=[wide, wide, wide, whole(sum_rows, size), square, square, square],
        out_shape=[
            jax.ShapeDtypeStruct((size, points), BF16),
            jax.ShapeDtypeStruct((size, points), F32),
            jax.ShapeDtypeStruct((size, points), BF16),
            jax.ShapeDtypeStruct((sum_rows, size), F32),
        ]
        + [jax.ShapeDtypeStruct((size, size), BF16)] * 3,
        scratch_shapes=[pltpu.VMEM((size, 2 * size), F32), pltpu.VMEM((size, 128), F32)],
        compiler_params=params,
    )(
        x, u, payload_linear_map, partition_chooser_map, partition_group_map, scale_row,
        final_linear_map,
    )
    sums = reduce_over(sums, n_point, False)
    att, dnum, dws, dmap = pl.pallas_call(
        functools.partial(token_kernel, heads),
        out_shape=[
            jax.ShapeDtypeStruct((size, size), BF16),
            jax.ShapeDtypeStruct((size, size), BF16),
            jax.ShapeDtypeStruct((size, 128), F32),
            jax.ShapeDtypeStruct((3, head, size), F32),
        ],
        compiler_params=pltpu.CompilerParams(vmem_limit_bytes=VMEM_LIMIT),
    )(sums, centroid_qkv_maps)
    resp, din, grads = pl.pallas_call(
        functools.partial(backward_kernel, heads, n_point),
        grid=(steps,),
        in_specs=[
            tall, tall, wide, wide, wide, square, square, whole(size, 128),
            square, square, square, square, whole(1, size), whole(3 * head, size),
        ],
        out_specs=[tall, tall, whole(grad_rows, size)],
        out_shape=[
            jax.ShapeDtypeStruct((points, size), BF16),
            jax.ShapeDtypeStruct((points, size), BF16),
            jax.ShapeDtypeStruct((grad_rows, size), F32),
        ],
        compiler_params=params,
    )(
        x, u, vt, wt, dmt, att, dnum, dws,
        wp, hi, lo, final_linear_map, final_shift_vector[None, :],
        dmap.reshape(3 * head, size),
    )
    grads = reduce_over(grads, n_point, True)
    scaling = 1.0 / math.sqrt(
        batch * points * lax.axis_size("point") * lax.axis_size("dp")
    )
    square_out = jax.ShapeDtypeStruct((size, size), F32)
    payload, chooser, group, maps, softness, final, shift = pl.pallas_call(
        functools.partial(finish_kernel, heads, scaling),
        out_shape=[
            square_out,
            square_out,
            jax.ShapeDtypeStruct((head, head), F32),
            jax.ShapeDtypeStruct((3 * head, head), F32),
            jax.ShapeDtypeStruct((1, heads), F32),
            square_out,
            jax.ShapeDtypeStruct((1, size), F32),
        ],
        compiler_params=pltpu.CompilerParams(vmem_limit_bytes=VMEM_LIMIT),
    )(grads, hi, lo, partition_chooser_map, partition_group_map, scale_row)
    return (
        resp.reshape(batch, points, size),
        din.reshape(batch, points, size),
        payload,
        chooser,
        group,
        maps.reshape(3, head, head),
        softness[0],
        final,
        shift[0],
    )


def solution(mesh):
    placed = (
        P(("groups", "dp"), "point", None),
        P(),
        P(),
        P(),
        P(),
        P(),
        P(),
        P(),
        P(("groups", "dp"), "point", None),
    )
    return jax.shard_map(
        shards,
        mesh=mesh,
        in_specs=placed,
        out_specs=(
            P(("groups", "dp"), "point", None),
            P(("groups", "dp"), "point", None),
            P("groups", None),
            P("groups", None),
            P("groups", None),
            P("groups", None, None),
            P("groups"),
            P("groups", None),
            P("groups"),
        ),
        check_vma=False,
    )
```

```python
import functools
import math

import jax
import jax.numpy as jnp
from jax import lax
from jax.experimental import pallas as pl
from jax.experimental.pallas import tpu as pltpu
from jax.sharding import PartitionSpec as P

EPS = 1e-05
HIGH = lax.Precision.HIGHEST
F32 = jnp.float32
BF16 = jnp.bfloat16
VMEM_LIMIT = 56 * 1024 * 1024


def nt(a, b, precision=None):
    return lax.dot_general(
        a, b, (((1,), (1,)), ((), ())), precision=precision, preferred_element_type=F32
    )


def nn(a, b, precision=None):
    return lax.dot_general(
        a, b, (((1,), (0,)), ((), ())), precision=precision, preferred_element_type=F32
    )


def tn(a, b, precision=None):
    return lax.dot_general(
        a, b, (((0,), (0,)), ((), ())), precision=precision, preferred_element_type=F32
    )


def block_mask(size, head):
    row = lax.broadcasted_iota(jnp.int32, (size, size), 0) // head
    col = lax.broadcasted_iota(jnp.int32, (size, size), 1) // head
    return row == col


def fold(square, mask, heads, head):
    kept = jnp.where(mask, square, 0.0)
    return jnp.sum(kept.reshape(heads, head, heads * head), axis=0)


def unfold(flat, mask, heads):
    return jnp.where(mask, jnp.concatenate([flat] * heads, axis=0), 0.0)


def pick(size, head, dtype):
    row = lax.broadcasted_iota(jnp.int32, (size, head), 0)
    col = lax.broadcasted_iota(jnp.int32, (size, head), 1)
    return jnp.where(row % head == col, 1.0, 0.0).astype(dtype)


def head_column(scale_row, size, head):
    heads = size // head
    row = lax.broadcasted_iota(jnp.int32, (size, heads), 0) // head
    mine = row == lax.broadcasted_iota(jnp.int32, (size, heads), 1)
    return jnp.sum(jnp.where(mine, scale_row, 0.0), axis=1, keepdims=True), mine


def square_transposed(group, size, head):
    e = pick(size, head, BF16)
    return jnp.where(block_mask(size, head), nt(nt(e, group).astype(BF16), e), 0.0)


def forward_kernel(
    heads, x_ref, u_ref, payload_ref, chooser_ref, group_ref, scale_ref, wf_ref,
    vt_ref, wt_ref, dmt_ref, sums_ref, hi_ref, lo_ref, hi_t_ref, lo_t_ref, wp_ref, acc, wacc
):
    step = pl.program_id(0)
    size, rows = wt_ref.shape
    head = size // heads

    @pl.when(step == 0)
    def _():
        row = lax.broadcasted_iota(jnp.int32, (size, size), 0)
        col = lax.broadcasted_iota(jnp.int32, (size, size), 1)
        same = jnp.where(row == col, 1.0, 0.0).astype(BF16)
        wp_ref[...] = nt(same, payload_ref[...]).astype(BF16)
        group_t = square_transposed(group_ref[...], size, head).astype(BF16)
        column, _ = head_column(scale_ref[...], size, head)
        joined = nt(group_t, chooser_ref[...]) / column
        high = joined.astype(BF16)
        hi_ref[...] = high
        low = joined - high.astype(F32)
        lo_ref[...] = low.astype(BF16)
        hi_t_ref[...] = joined.T.astype(BF16)
        lo_t_ref[...] = low.T.astype(BF16)

    x = x_ref[...]
    values = nt(wp_ref[...], x).astype(BF16)
    logit = nt(hi_ref[...], x) + nt(lo_ref[...], x)
    d_mixed = nt(wf_ref[...], u_ref[...]).astype(BF16)
    logit = logit.reshape(heads, head, rows)
    top = jnp.max(logit, axis=1, keepdims=True)
    grown = jnp.exp(logit - top)
    share = 1.0 / jnp.sum(grown, axis=1, keepdims=True)
    weights = (grown * share).reshape(size, rows)
    weights_bf = weights.astype(BF16)
    vt_ref[...] = values
    dmt_ref[...] = d_mixed
    wt_ref[...] = weights
    both = nt(weights_bf, jnp.concatenate([values, d_mixed], axis=0))
    lanes = wacc.shape[1]
    part = weights[:, :lanes]
    for i in range(1, rows // lanes):
        part = part + weights[:, i * lanes : (i + 1) * lanes]

    @pl.when(step == 0)
    def _():
        acc[...] = both
        wacc[...] = part

    @pl.when(step > 0)
    def _():
        acc[...] += both
        wacc[...] += part

    @pl.when(step == pl.num_programs(0) - 1)
    def _():
        mask = block_mask(size, head)
        total = jnp.sum(wacc[...], axis=1, keepdims=True)
        sums_ref[0:head, :] = fold(acc[:, :size], mask, heads, head)
        sums_ref[head : 2 * head, :] = fold(acc[:, size:], mask, heads, head)
        sums_ref[2 * head : 3 * head, :] = fold(
            jnp.broadcast_to(total, (size, size)), mask, heads, head
        )
        spare = sums_ref.shape[0] - 3 * head
        if spare:
            sums_ref[3 * head :, :] = jnp.zeros((spare, size), F32)


def token_kernel(heads, sums_ref, maps_ref, att_ref, dnum_ref, dws_ref, dmap_ref):
    size = sums_ref.shape[1]
    head = size // heads
    mask = block_mask(size, head)
    numerator = unfold(sums_ref[0:head, :], mask, heads)
    d_att = unfold(sums_ref[head : 2 * head, :], mask, heads)
    spread = unfold(sums_ref[2 * head : 3 * head, :], mask, heads)
    weight_sum = jnp.sum(spread, axis=1, keepdims=True) * (1.0 / head)
    reciprocal = 1.0 / (weight_sum + EPS)
    tokens = numerator * reciprocal
    e = pick(size, head, BF16)
    maps = [
        jnp.where(mask, nt(nn(e, maps_ref[i]).astype(BF16), e), 0.0) for i in range(3)
    ]
    q, k, v = (nn(tokens, w, HIGH) for w in maps)
    root = 1.0 / math.sqrt(head)
    scores = jnp.where(mask, nt(q, k, HIGH) * root, -jnp.inf)
    grown = jnp.exp(scores - jnp.max(scores, axis=1, keepdims=True))
    probs = grown / jnp.sum(grown, axis=1, keepdims=True)
    attended = nn(probs, v, HIGH)
    d_v = tn(probs, d_att, HIGH)
    d_probs = nt(d_att, v, HIGH)
    d_scores = probs * (d_probs - jnp.sum(probs * d_probs, axis=1, keepdims=True)) * root
    d_q = nn(d_scores, k, HIGH)
    d_k = tn(d_scores, q, HIGH)
    d_tokens = nt(d_q, maps[0], HIGH) + nt(d_k, maps[1], HIGH) + nt(d_v, maps[2], HIGH)
    att_ref[...] = attended.astype(BF16)
    dnum_ref[...] = (d_tokens * reciprocal).astype(BF16)
    dws = -jnp.sum(d_tokens * tokens, axis=1, keepdims=True) * reciprocal
    dws_ref[...] = jnp.broadcast_to(dws, dws_ref.shape)
    for i, d in enumerate((d_q, d_k, d_v)):
        dmap_ref[i] = fold(tn(tokens, d, HIGH), mask, heads, head)


def backward_kernel(
    heads, points,
    x_ref, u_ref, vt_ref, wt_ref, dmt_ref, att_ref, dnum_ref, dws_ref,
    payload_ref, hi_t_ref, lo_t_ref, wf_ref, shift_ref, dmap_ref,
    resp_ref, din_ref, grads_ref,
):
    step = pl.program_id(0)
    size, rows = wt_ref.shape
    head = size // heads
    u = u_ref[...]
    x = x_ref[...]
    weights = wt_ref[...]
    weights_bf = weights.astype(BF16)
    mixed = tn(att_ref[...], weights_bf).astype(BF16)
    d_values = tn(dnum_ref[...], weights_bf).astype(BF16)
    resp_ref[...] = (tn(mixed, wf_ref[...]) + shift_ref[...]).astype(BF16)
    d_weights = nn(att_ref[...], dmt_ref[...]) + nn(dnum_ref[...], vt_ref[...])
    d_weights = d_weights + dws_ref[:, 0:1]
    product = (weights * d_weights).reshape(heads, head, rows)
    mean = jnp.sum(product, axis=1, keepdims=True)
    d_logit = (product - weights.reshape(heads, head, rows) * mean).reshape(size, rows)
    d_high = d_logit.astype(BF16)
    d_low = (d_logit - d_high.astype(F32)).astype(BF16)
    d_input = (
        nn(payload_ref[...], d_values)
        + nn(hi_t_ref[...], d_high)
        + nn(lo_t_ref[...], d_high)
        + nn(hi_t_ref[...], d_low)
    )
    din_ref[...] = d_input.astype(BF16).T
    ones = jnp.ones((8, rows), BF16)
    parts = (nn(d_values, x), nn(d_high, x) + nn(d_low, x), nn(mixed, u), nn(ones, u))
    spans = ((0, size), (size, 2 * size), (2 * size, 3 * size), (3 * size, 3 * size + 8))

    @pl.when(step == 0)
    def _():
        for (a, b), part in zip(spans, parts):
            grads_ref[a:b, :] = part
        tail = 3 * size + 8
        end = tail + 3 * head
        grads_ref[tail:end, :] = dmap_ref[...] * (1.0 / points)
        spare = grads_ref.shape[0] - end
        if spare:
            grads_ref[end:, :] = jnp.zeros((spare, size), F32)

    @pl.when(step > 0)
    def _():
        for (a, b), part in zip(spans, parts):
            grads_ref[a:b, :] += part


def reduce_kernel(n, paired, x_ref, out_ref, recv, full, rs_sem, ag_sem, *more):
    me = lax.axis_index("point")
    core = lax.axis_index("dp")
    peers = [lax.rem(me + o, n) for o in range(1, n)]
    mesh_id = pl.DeviceIdType.MESH
    barrier = pltpu.get_barrier_semaphore()
    for peer in peers:
        pl.semaphore_signal(barrier, inc=1, device_id={"point": peer}, device_id_type=mesh_id)
    if paired:
        pl.semaphore_signal(barrier, inc=1, device_id={"dp": 1 - core}, device_id_type=mesh_id)
    pl.semaphore_wait(barrier, n if paired else n - 1)

    def send(src, dst, sems, slot, target):
        copy = pltpu.make_async_remote_copy(
            src_ref=src, dst_ref=dst, send_sem=sems.at[0, slot], recv_sem=sems.at[1, slot],
            device_id=target, device_id_type=mesh_id,
        )
        copy.start()
        return copy

    if paired:
        swapped, half, swap_sem, pass_sem = more
        swaps = [
            send(x_ref.at[1 - core, k], swapped.at[k], swap_sem, i, {"dp": 1 - core})
            for i, k in enumerate(peers + [me])
        ]
        source, target = half, full.at[core]
    else:
        source, target = x_ref, full
    scatter = []
    for o, peer in enumerate(peers):
        if paired:
            swaps[o].wait_recv()
            half[peer] = x_ref[core, peer] + swapped[peer]
        scatter.append(send(source.at[peer], recv.at[o], rs_sem, o, {"point": peer}))
    if paired:
        swaps[n - 1].wait_recv()
        total = x_ref[core, me] + swapped[me]
    else:
        total = source[me]
    for o, copy in enumerate(scatter):
        copy.wait_recv()
        total = total + recv[o]
    target[me] = total
    gather = [
        send(target.at[me], target.at[me], ag_sem, o, {"point": peer})
        for o, peer in enumerate(peers)
    ]
    passed = []
    if paired:
        passed.append(send(target.at[me], target.at[me], pass_sem, 0, {"dp": 1 - core}))
    for o, copy in enumerate(gather):
        copy.wait_recv()
        if paired:
            owner = lax.rem(me + n - (o + 1), n)
            passed.append(
                send(target.at[owner], target.at[owner], pass_sem, o + 1, {"dp": 1 - core})
            )
    if paired:
        for copy in passed:
            copy.wait_recv()
        for copy in swaps + passed:
            copy.wait_send()
    for copy in scatter + gather:
        copy.wait_send()
    out_ref[...] = full[...]


def reduce_over(x, n, paired):
    rows, size = x.shape
    r = rows // (2 * n if paired else n)
    shape = (2, n, r, size) if paired else (n, r, size)
    dma = pltpu.SemaphoreType.DMA
    scratch = [
        pltpu.VMEM((n - 1, r, size), F32), pltpu.VMEM(shape, F32), dma((2, n - 1)), dma((2, n - 1)),
    ]
    if paired:
        scratch += [
            pltpu.VMEM((n, r, size), F32), pltpu.VMEM((n, r, size), F32), dma((2, n)), dma((2, n)),
        ]
    out = pl.pallas_call(
        functools.partial(reduce_kernel, n, paired),
        out_shape=jax.ShapeDtypeStruct(shape, F32),
        in_specs=[pl.BlockSpec(memory_space=pltpu.VMEM)],
        out_specs=pl.BlockSpec(memory_space=pltpu.VMEM),
        scratch_shapes=scratch,
        compiler_params=pltpu.CompilerParams(
            collective_id=1 if paired else 0, has_side_effects=True, vmem_limit_bytes=VMEM_LIMIT
        ),
    )(x.reshape(shape))
    return out.reshape(rows, size)


def padded(rows, pieces):
    return pieces * 8 * -(-rows // (pieces * 8))


def finish_kernel(
    heads, scaling, grads_ref, hi_ref, lo_ref, chooser_ref, group_ref, scale_ref,
    payload_out, chooser_out, group_out, maps_out, softness_out, final_out, shift_out,
):
    size = grads_ref.shape[1]
    head = size // heads
    mask = block_mask(size, head)
    e = pick(size, head, F32)
    payload_out[...] = grads_ref[0:size, :].T * scaling
    logit_deriv = grads_ref[size : 2 * size, :]
    column, mine = head_column(scale_ref[...], size, head)
    raw_deriv = logit_deriv * (scaling / column)
    group_t = square_transposed(group_ref[...], size, head)
    chooser_out[...] = tn(raw_deriv, group_t, HIGH)
    crossed = jnp.where(mask, nn(raw_deriv, chooser_ref[...].astype(F32), HIGH), 0.0)
    group_out[...] = tn(e, tn(crossed, e, HIGH), HIGH)
    joined = hi_ref[...].astype(F32) + lo_ref[...].astype(F32)
    per_row = jnp.sum(joined * logit_deriv, axis=1, keepdims=True)
    per_head = jnp.sum(jnp.where(mine, per_row, 0.0), axis=0, keepdims=True)
    softness_out[...] = -scaling * per_head / scale_ref[...]
    final_out[...] = grads_ref[2 * size : 3 * size, :] * scaling
    shift_out[...] = grads_ref[3 * size : 3 * size + 1, :] * scaling
    tail = 3 * size + 8
    maps_out[...] = nn(grads_ref[tail : tail + 3 * head, :], e, HIGH) * scaling


def shards(
    mesh_signals,
    payload_linear_map,
    partition_chooser_map,
    partition_group_map,
    softness_scale,
    centroid_qkv_maps,
    final_linear_map,
    final_shift_vector,
    upstream_adjoint,
):
    batch, points, size = mesh_signals.shape
    heads = softness_scale.shape[0]
    head = size // heads
    x = mesh_signals.reshape(points, size)
    u = upstream_adjoint.reshape(points, size)
    rows = 512
    steps = points // rows
    n_point = lax.axis_size("point")
    sum_rows = padded(3 * head, n_point)
    grad_rows = padded(3 * size + 8 + 3 * head, 2 * n_point)
    scale_row = softness_scale[None, :]
    params = pltpu.CompilerParams(
        dimension_semantics=("arbitrary",), vmem_limit_bytes=VMEM_LIMIT
    )
    tall = pl.BlockSpec((rows, size), lambda i: (i, 0))
    wide = pl.BlockSpec((size, rows), lambda i: (0, i))

    def whole(*shape):
        return pl.BlockSpec(shape, lambda i: (0,) * len(shape))

    square = whole(size, size)
    vt, wt, dmt, sums, hi, lo, hi_t, lo_t = pl.pallas_call(
        functools.partial(forward_kernel, heads),
        grid=(steps,),
        in_specs=[
            tall, tall, square, square, whole(head, head), whole(1, heads), square,
        ],
        out_specs=[wide, wide, wide, whole(sum_rows, size)] + [square] * 4,
        out_shape=[
            jax.ShapeDtypeStruct((size, points), BF16),
            jax.ShapeDtypeStruct((size, points), F32),
            jax.ShapeDtypeStruct((size, points), BF16),
            jax.ShapeDtypeStruct((sum_rows, size), F32),
        ]
        + [jax.ShapeDtypeStruct((size, size), BF16)] * 4,
        scratch_shapes=[
            pltpu.VMEM((size, size), BF16),
            pltpu.VMEM((size, 2 * size), F32),
            pltpu.VMEM((size, 128), F32),
        ],
        compiler_params=params,
    )(
        x, u, payload_linear_map, partition_chooser_map, partition_group_map, scale_row,
        final_linear_map,
    )
    sums = reduce_over(sums, n_point, False)
    att, dnum, dws, dmap = pl.pallas_call(
        functools.partial(token_kernel, heads),
        out_shape=[
            jax.ShapeDtypeStruct((size, size), BF16),
            jax.ShapeDtypeStruct((size, size), BF16),
            jax.ShapeDtypeStruct((size, 128), F32),
            jax.ShapeDtypeStruct((3, head, size), F32),
        ],
        compiler_params=pltpu.CompilerParams(vmem_limit_bytes=VMEM_LIMIT),
    )(sums, centroid_qkv_maps)
    resp, din, grads = pl.pallas_call(
        functools.partial(backward_kernel, heads, n_point),
        grid=(steps,),
        in_specs=[
            tall, tall, wide, wide, wide, square, square, whole(size, 128),
            square, square, square, square, whole(1, size), whole(3 * head, size),
        ],
        out_specs=[tall, tall, whole(grad_rows, size)],
        out_shape=[
            jax.ShapeDtypeStruct((points, size), BF16),
            jax.ShapeDtypeStruct((points, size), BF16),
            jax.ShapeDtypeStruct((grad_rows, size), F32),
        ],
        compiler_params=params,
    )(
        x, u, vt, wt, dmt, att, dnum, dws,
        payload_linear_map, hi_t, lo_t, final_linear_map, final_shift_vector[None, :],
        dmap.reshape(3 * head, size),
    )
    grads = reduce_over(grads, n_point, True)
    scaling = 1.0 / math.sqrt(
        batch * points * lax.axis_size("point") * lax.axis_size("dp")
    )
    square_out = jax.ShapeDtypeStruct((size, size), F32)
    payload, chooser, group, maps, softness, final, shift = pl.pallas_call(
        functools.partial(finish_kernel, heads, scaling),
        out_shape=[
            square_out,
            square_out,
            jax.ShapeDtypeStruct((head, head), F32),
            jax.ShapeDtypeStruct((3 * head, head), F32),
            jax.ShapeDtypeStruct((1, heads), F32),
            square_out,
            jax.ShapeDtypeStruct((1, size), F32),
        ],
        compiler_params=pltpu.CompilerParams(vmem_limit_bytes=VMEM_LIMIT),
    )(grads, hi, lo, partition_chooser_map, partition_group_map, scale_row)
    return (
        resp.reshape(batch, points, size),
        din.reshape(batch, points, size),
        payload,
        chooser,
        group,
        maps.reshape(3, head, head),
        softness[0],
        final,
        shift[0],
    )


def solution(mesh):
    placed = (
        P(("groups", "dp"), "point", None),
        P(),
        P(),
        P(),
        P(),
        P(),
        P(),
        P(),
        P(("groups", "dp"), "point", None),
    )
    return jax.shard_map(
        shards,
        mesh=mesh,
        in_specs=placed,
        out_specs=(
            P(("groups", "dp"), "point", None),
            P(("groups", "dp"), "point", None),
            P("groups", None),
            P("groups", None),
            P("groups", None),
            P("groups", None, None),
            P("groups"),
            P("groups", None),
            P("groups"),
        ),
        check_vma=False,
    )
```
